128 devices in a mesh: replica: 4 (over z), shard: 32 (over x, y, core).
Axes of the slice: x: 4, y: 4, z: 4, core: 2. Of those that a mesh axis runs over, the one named last changes fastest.
Arguments:
- grads: bfloat16 [4, 2048, 28672], P('replica', 'shard'), may hold values from -3 to 3
- owner_map: int32 [4, 56], replicated, may hold values from 0 to 95, as said below
- factor_left: float32 [128, 3, 512, 512], P(('replica', 'shard')), may hold values from -1 to 7
- factor_right: float32 [128, 3, 512, 512], P(('replica', 'shard')), may hold values from -1 to 7
- left_inverse_roots: bfloat16 [128, 3, 512, 512], P(('replica', 'shard')), may hold values from -1 to 7
- right_inverse_roots: bfloat16 [128, 3, 512, 512], P(('replica', 'shard')), may hold values from -1 to 7
Outputs:
- new_left: float32 [128, 3, 512, 512], P(('replica', 'shard'))
- new_right: float32 [128, 3, 512, 512], P(('replica', 'shard'))
- update: bfloat16 [2048, 28672], P('shard')
The draws below stay inside these ranges and needn't reach their ends.
Inputs may be any that keep to these rules, and one draw needn't show every extreme that they name: `owner_map`: within one block row and one replica's 14 block columns no two blocks name the same owner; within one replica's 14 block columns no two blocks share an entry; some owner holds 3 blocks in every draw.
All inputs are finite; a program needn't handle non-finite values.
Results may differ from the reference program's by a relative error of at most 0.0058.
Values may be sent and summed in bfloat16 or wider, within the bound.
No kernel may reach another device: no remote copies, remote signals or barrier semaphores. Data moves between devices by JAX's collectives and lax.ppermute only.
A program may use at most 128 MiB of HBM per device.

```python
import math
import jax
import jax.numpy as jnp
from jax import lax

BS = 512
BR = 4
CAP = 3
REPLICAS = 4
SHARDS = 32
FACTOR_OWNERS = 128
NBC = 56
COLS = 28672
ROWS = 2048


def assemble(key_diag, offdiag, floor_scale, top_scale, spread):
    diagonal = jnp.exp(jax.random.uniform(key_diag, (FACTOR_OWNERS, CAP, BS, 1), jnp.float32, math.log(floor_scale), math.log(top_scale)))
    identity = jnp.eye(BS, dtype=jnp.float32)
    return diagonal * identity + offdiag * (spread / math.sqrt(BS))


def draw_owner_map(key, part):
    key = jax.random.fold_in(key, 7)
    per_group = NBC // REPLICAS
    stride = (per_group + 2) // 3
    columns_list = []
    for group_index in range(REPLICAS):
        middle = jax.random.permutation(jax.random.fold_in(key, 100 + group_index), SHARDS - 2).astype(jnp.int32) + 1
        first = jnp.zeros((1,), jnp.int32)
        last = jnp.full((1,), SHARDS - 1, jnp.int32)
        owners = jnp.concatenate([first, middle[:2 * stride - 1], last, middle[2 * stride - 1:]])
        row_list = []
        for row_index in range(BR):
            ordering = jax.random.permutation(jax.random.fold_in(key, 1000 + group_index * BR + row_index), per_group)
            position = row_index * stride + ordering
            counted = jnp.zeros((per_group,), jnp.int32)
            for earlier in range(row_index):
                counted = counted + (position < earlier * stride + per_group).astype(jnp.int32)
            row_list.append(owners[position] * CAP + counted)
        columns_list.append(jnp.stack(row_list))
    return jnp.concatenate(columns_list, axis=1).astype(jnp.int32)


def draw_factor_left(key, part):
    key = jax.random.fold_in(key, 3)
    key_diag, key_off = jax.random.split(key)
    full_shape = (FACTOR_OWNERS, CAP, BS, BS)
    offdiag = jnp.clip(jax.random.normal(key_off, full_shape, jnp.float32), -4.0, 4.0)
    return assemble(key_diag, offdiag, 0.5, 3.0, 0.3)


def draw_factor_right(key, part):
    key = jax.random.fold_in(key, 4)
    key_diag, key_off = jax.random.split(key)
    full_shape = (FACTOR_OWNERS, CAP, BS, BS)
    offdiag = jnp.clip(jax.random.normal(key_off, full_shape, jnp.float32), -4.0, 4.0)
    return assemble(key_diag, offdiag, 0.5, 3.0, 0.3)


def draw_left_inverse_roots(key, part):
    key = jax.random.fold_in(key, 5)
    key_diag, key_off = jax.random.split(key)
    full_shape = (FACTOR_OWNERS, CAP, BS, BS)
    offdiag = jnp.clip(jax.random.normal(key_off, full_shape, jnp.float32), -4.0, 4.0)
    return assemble(key_diag, offdiag, 0.5, 2.0, 0.6).astype(jnp.bfloat16)


def draw_right_inverse_roots(key, part):
    key = jax.random.fold_in(key, 6)
    key_diag, key_off = jax.random.split(key)
    full_shape = (FACTOR_OWNERS, CAP, BS, BS)
    offdiag = jnp.clip(jax.random.normal(key_off, full_shape, jnp.float32), -4.0, 4.0)
    return assemble(key_diag, offdiag, 0.5, 2.0, 0.6).astype(jnp.bfloat16)


def block_levels(key, shape, shards, low, largest):
    factor_of = 1.0
    for dim, parts in shards:
        steps = jax.random.uniform(jax.random.fold_in(jax.random.fold_in(key, 6), dim), (parts,), jnp.float32, low / len(shards), largest / len(shards))
        factor_of = factor_of * jnp.repeat(jnp.exp(steps), shape[dim] // parts).reshape((-1,) + (1,) * (len(shape) - 1 - dim))
    return factor_of


def bell_draw(own_key, shape, scale, limit, shards=(), held_as=jnp.bfloat16):
    values = scale * jax.random.normal(own_key, shape, jnp.float32)
    if shards:
        values = values * block_levels(own_key, shape, shards, -0.22, 0.18)
    return jnp.clip(values, -limit, limit).astype(held_as)


def setup_inputs(seed: int = 0) -> dict:
    arg_keys = jax.random.split(jax.random.key(seed), 7)
    return {
        "grads": bell_draw(arg_keys[0], (REPLICAS, ROWS, COLS), 0.5, 3.0, ((0, 4), (1, 32))),
        "owner_map": draw_owner_map(jax.random.fold_in(arg_keys[6], 71), 0),
        "factor_left": draw_factor_left(jax.random.fold_in(arg_keys[6], 71), 0),
        "factor_right": draw_factor_right(jax.random.fold_in(arg_keys[6], 71), 0),
        "left_inverse_roots": draw_left_inverse_roots(jax.random.fold_in(arg_keys[6], 71), 0),
        "right_inverse_roots": draw_right_inverse_roots(jax.random.fold_in(arg_keys[6], 71), 0),
    }


def reference(grads, owner_map, factor_left, factor_right, left_inverse_roots, right_inverse_roots):
    summed = jnp.sum(grads.astype(jnp.float32), axis=0)
    blocks = summed.astype(jnp.bfloat16).reshape(BR, BS, NBC, BS).transpose(0, 2, 1, 3).reshape(BR * NBC, BS, BS)
    per_group = NBC // REPLICAS
    column_ids = jnp.arange(NBC, dtype=jnp.int32)
    owner_dev = (column_ids[None, :] // per_group) * SHARDS + owner_map // CAP
    slot_index = (owner_dev * CAP + owner_map % CAP).reshape(-1).astype(jnp.int32)
    left_flat = factor_left.reshape(FACTOR_OWNERS * CAP, BS, BS)
    flattened_right = factor_right.reshape(FACTOR_OWNERS * CAP, BS, BS)
    rootl_flat = left_inverse_roots.reshape(FACTOR_OWNERS * CAP, BS, BS)
    rootr_flat = right_inverse_roots.reshape(FACTOR_OWNERS * CAP, BS, BS)

    def per_block(operand):
        block_grad, where = operand
        left_gram_matrix = jnp.dot(block_grad, block_grad.T, preferred_element_type=jnp.float32)
        right_gram_matrix = jnp.dot(block_grad.T, block_grad, preferred_element_type=jnp.float32)
        preconditioned_update = jnp.dot(rootl_flat[where], block_grad, preferred_element_type=jnp.float32).astype(jnp.bfloat16)
        product = jnp.dot(preconditioned_update, rootr_flat[where], preferred_element_type=jnp.float32).astype(jnp.bfloat16)
        return left_gram_matrix, right_gram_matrix, product

    left_gram_matrix, right_gram_matrix, product = lax.map(per_block, (blocks, slot_index))
    new_left = (0.9 * left_flat).at[slot_index].add((0.1 / BS) * left_gram_matrix)
    new_right = (0.9 * flattened_right).at[slot_index].add((0.1 / BS) * right_gram_matrix)
    update = product.reshape(BR, NBC, BS, BS).transpose(0, 2, 1, 3).reshape(BR * BS, NBC * BS)
    return (new_left.reshape(FACTOR_OWNERS, CAP, BS, BS), new_right.reshape(FACTOR_OWNERS, CAP, BS, BS), update)
```

```python
import functools

import jax
import jax.numpy as jnp
from jax import lax
from jax.experimental import pallas as pl
from jax.experimental.pallas import tpu as pltpu
from jax.sharding import PartitionSpec as P

FORWARD = (64,)
BACKWARD = (64,)


def offsets(parts):
    return [sum(parts[:at]) for at in range(len(parts))]


def any_spec():
    return pl.BlockSpec(memory_space=pl.ANY)


def vmem_spec():
    return pl.BlockSpec(memory_space=pltpu.VMEM)


def params():
    return pltpu.CompilerParams(vmem_limit_bytes=48 * 1024 * 1024)


def slot_kernel(block_size, owners, own, left, right, out, held, sems):
    count = held.shape[0]
    copies = []
    for at in range(count):
        columns = slice(at * block_size, (at + 1) * block_size)
        total = (
            own[:, columns].astype(jnp.float32)
            + left[:, columns].astype(jnp.float32)
            + right[:, columns].astype(jnp.float32)
        )
        held[at] = total.astype(jnp.bfloat16)
        copy = pltpu.make_async_copy(held.at[at], out.at[owners[at]], sems.at[at])
        copy.start()
        copies.append(copy)
    for copy in copies:
        copy.wait()


def to_slots(owners, own, left, right, num_shards, block_size):
    rows, columns = own.shape
    count = columns // block_size
    return pl.pallas_call(
        functools.partial(slot_kernel, block_size),
        out_shape=jax.ShapeDtypeStruct((num_shards, rows, block_size), jnp.bfloat16),
        in_specs=[pl.BlockSpec(memory_space=pltpu.SMEM)] + [vmem_spec()] * 3,
        out_specs=any_spec(),
        scratch_shapes=[
            pltpu.VMEM((count, rows, block_size), jnp.bfloat16),
            pltpu.SemaphoreType.DMA((count,)),
        ],
        compiler_params=params(),
        cost_estimate=pl.CostEstimate(
            flops=3 * rows * columns, bytes_accessed=8 * rows * columns, transcendentals=0
        ),
        name="to_slots",
    )(owners, own, left, right)


def whole_block(parts):
    joined = jnp.concatenate([part[0] for part in parts], axis=1)
    return joined.reshape(joined.shape[0] * joined.shape[1], joined.shape[2])


def update_kernel(num_parts, bounds, rows_of, *refs):
    parts = refs[:num_parts]
    left_root, right_root = refs[num_parts], refs[num_parts + 1]
    outs = refs[num_parts + 2 :]
    block = whole_block(parts)
    applied = jnp.dot(left_root[0], block, preferred_element_type=jnp.float32).astype(jnp.bfloat16)
    product = jnp.dot(applied, right_root[0], preferred_element_type=jnp.float32).astype(jnp.bfloat16)
    product = product.reshape(parts[0].shape[1], -1, product.shape[1])
    for out, (start, rows) in zip(outs, bounds, strict=True):
        out[0] = product[:, start : start + rows]


def updates(rows_of, parts, left_roots, right_roots, back):
    capacity, block_size = left_roots.shape[0], left_roots.shape[1]
    block_rows, strips = parts[0].shape[:2]
    bounds = list(zip(offsets(back), back, strict=True))
    at_row = lambda t, rows_of: (rows_of[t], 0, 0, 0)
    root = pl.BlockSpec((1, block_size, block_size), lambda t, rows_of: (t, 0, 0))
    return pl.pallas_call(
        functools.partial(update_kernel, len(parts), bounds),
        grid_spec=pltpu.PrefetchScalarGridSpec(
            num_scalar_prefetch=1,
            grid=(capacity,),
            in_specs=[pl.BlockSpec((1,) + part.shape[1:], at_row) for part in parts] + [root, root],
            out_specs=[pl.BlockSpec((1, strips, rows, block_size), at_row) for rows in back],
        ),
        out_shape=[
            jax.ShapeDtypeStruct((block_rows, strips, rows, block_size), jnp.bfloat16)
            for rows in back
        ],
        compiler_params=params(),
        cost_estimate=pl.CostEstimate(
            flops=4 * capacity * block_size**3,
            bytes_accessed=8 * capacity * block_size**2,
            transcendentals=0,
        ),
        name="updates",
    )(rows_of, *parts, left_roots, right_roots)


def gram_kernel(num_parts, rows_of, named, *refs):
    parts = refs[:num_parts]
    left, right, new_left, new_right = refs[num_parts:]
    block = whole_block(parts)
    size = block.shape[0]
    holds = named[pl.program_id(0)] > 0
    scale = 0.1 / size
    gram = lax.dot_general(block, block, (((1,), (1,)), ((), ())), preferred_element_type=jnp.float32)
    new_left[0] = 0.9 * left[0] + jnp.where(holds, scale * gram, 0.0)
    gram = lax.dot_general(block, block, (((0,), (0,)), ((), ())), preferred_element_type=jnp.float32)
    new_right[0] = 0.9 * right[0] + jnp.where(holds, scale * gram, 0.0)


def statistics(rows_of, named, parts, factor_left, factor_right):
    capacity, block_size = factor_left.shape[0], factor_left.shape[1]
    at_row = lambda t, rows_of, named: (rows_of[t], 0, 0, 0)
    square = pl.BlockSpec((1, block_size, block_size), lambda t, rows_of, named: (t, 0, 0))
    return pl.pallas_call(
        functools.partial(gram_kernel, len(parts)),
        grid_spec=pltpu.PrefetchScalarGridSpec(
            num_scalar_prefetch=2,
            grid=(capacity,),
            in_specs=[pl.BlockSpec((1,) + part.shape[1:], at_row) for part in parts]
            + [square, square],
            out_specs=[square, square],
        ),
        out_shape=[jax.ShapeDtypeStruct(factor_left.shape, jnp.float32)] * 2,
        compiler_params=params(),
        cost_estimate=pl.CostEstimate(
            flops=4 * capacity * block_size**3,
            bytes_accessed=18 * capacity * block_size**2,
            transcendentals=0,
        ),
        name="statistics",
    )(rows_of, named, *parts, factor_left, factor_right)


def pick_kernel(block_size, count, owners, slots, out, sems):
    copies = []
    for at in range(count):
        columns = pl.ds(at * block_size, block_size)
        copy = pltpu.make_async_copy(slots.at[owners[at]], out.at[:, columns], sems.at[at])
        copy.start()
        copies.append(copy)
    for copy in copies:
        copy.wait()


def from_slots(owners, slots):
    count = owners.shape[0]
    _, rows, block_size = slots.shape
    return pl.pallas_call(
        functools.partial(pick_kernel, block_size, count),
        out_shape=jax.ShapeDtypeStruct((rows, count * block_size), jnp.bfloat16),
        in_specs=[pl.BlockSpec(memory_space=pltpu.SMEM), any_spec()],
        out_specs=any_spec(),
        scratch_shapes=[pltpu.SemaphoreType.DMA((count,))],
        compiler_params=params(),
        cost_estimate=pl.CostEstimate(
            flops=0, bytes_accessed=4 * rows * count * block_size, transcendentals=0
        ),
        name="from_slots",
    )(owners, slots)


def place_kernel(start, groups, own, left, right, far_left, far_right, *rest):
    out, sems = rest[-2:]
    rows, width = own.shape
    half = far_left.shape[1]
    copies = []
    for at, (piece, group, shift) in enumerate(
        ((own, 0, 0), (left, 1, 0), (right, 2, 0), (far_left, 3, 0), (far_right, 3, half))
    ):
        first = pl.multiple_of(groups[group] * width + shift, 128)
        copy = pltpu.make_async_copy(
            piece, out.at[pl.ds(start, rows), pl.ds(first, piece.shape[1])], sems.at[at]
        )
        copy.start()
        copies.append(copy)
    for copy in copies:
        copy.wait()


def place(groups, pieces, start, shape, held):
    given = () if held is None else (held,)
    return pl.pallas_call(
        functools.partial(place_kernel, start),
        out_shape=jax.ShapeDtypeStruct(shape, jnp.bfloat16),
        in_specs=[pl.BlockSpec(memory_space=pltpu.SMEM)] + [any_spec()] * (5 + len(given)),
        out_specs=any_spec(),
        scratch_shapes=[pltpu.SemaphoreType.DMA((5,))],
        input_output_aliases={} if held is None else {6: 0},
        compiler_params=params(),
        cost_estimate=pl.CostEstimate(
            flops=0, bytes_accessed=4 * pieces[0].shape[0] * shape[1], transcendentals=0
        ),
        name="place",
    )(groups, *pieces, *given)


def body(grads, owner_map, factor_left, factor_right, left_inverse_roots, right_inverse_roots):
    num_replicas = lax.axis_size("replica")
    num_shards = lax.axis_size("shard")
    replica_at = lax.axis_index("replica")
    shard_at = lax.axis_index("shard")
    strip_rows, columns = grads.shape[1], grads.shape[2]
    capacity, block_size = factor_left.shape[1], factor_left.shape[2]
    block_rows, block_cols = owner_map.shape
    per_group = block_cols // num_replicas
    width = per_group * block_size
    strips = block_size // strip_rows
    onward = [(at, (at + 1) % num_replicas) for at in range(num_replicas)]
    back = [(at, (at - 1) % num_replicas) for at in range(num_replicas)]
    to_right = lambda a: lax.ppermute(a, "replica", onward)
    to_left = lambda a: lax.ppermute(a, "replica", back)
    right_at = (replica_at + 1) % num_replicas
    left_at = (replica_at + num_replicas - 1) % num_replicas
    far_at = (replica_at + 2) % num_replicas

    group_entries = lax.dynamic_slice_in_dim(owner_map, replica_at * per_group, per_group, 1)
    row_entries = lax.dynamic_index_in_dim(group_entries, shard_at // strips, 0, keepdims=False)
    owners = row_entries // capacity
    targets = shard_at * capacity + jnp.arange(capacity, dtype=jnp.int32)
    match = jnp.any(group_entries[None] == targets[:, None, None], axis=2)
    named = jnp.any(match, axis=1)
    unused = jnp.logical_not(jnp.any(match, axis=0))
    rank_slot = jnp.cumsum(jnp.logical_not(named).astype(jnp.int32))
    rank_row = jnp.cumsum(unused.astype(jnp.int32))
    spare = jnp.logical_and(
        jnp.logical_and(jnp.logical_not(named)[:, None], unused[None]),
        rank_slot[:, None] == rank_row[None],
    )
    chosen = jnp.logical_or(match, spare)
    rows_of = jnp.sum(
        jnp.where(chosen, jnp.arange(block_rows, dtype=jnp.int32)[None], 0), axis=1
    ).astype(jnp.int32)
    named = named.astype(jnp.int32)

    tile = 8
    view = grads[0].reshape(strip_rows // tile, tile, num_replicas, width).transpose(0, 2, 1, 3)

    def piece(group, start, rows):
        part = lax.dynamic_slice(
            view, (start // tile, group, 0, 0), (rows // tile, 1, tile, width)
        )
        return part.reshape(rows, width)

    arrived = []
    for start, rows in zip(offsets(FORWARD), FORWARD, strict=True):
        half = rows // 2
        passed_right = to_right(piece(far_at, start, half))
        passed_left = to_left(piece(far_at, start + half, half))
        ahead = piece(right_at, start, rows)
        behind = piece(left_at, start, rows)
        add = lambda a, b: (a.astype(jnp.float32) + b.astype(jnp.float32)).astype(jnp.bfloat16)
        from_left = to_right(jnp.concatenate([add(ahead[:half], passed_right), ahead[half:]]))
        from_right = to_left(jnp.concatenate([behind[:half], add(behind[half:], passed_left)]))
        slots = to_slots(
            owners, piece(replica_at, start, rows), from_left, from_right, num_shards, block_size
        )
        came = lax.all_to_all(slots, "shard", split_axis=0, concat_axis=0, tiled=True)
        arrived.append(came.reshape(block_rows, strips, rows, block_size))

    outs = updates(rows_of, arrived, left_inverse_roots[0], right_inverse_roots[0], BACKWARD)
    new_left, new_right = statistics(rows_of, named, arrived, factor_left[0], factor_right[0])

    update = None
    groups = jnp.stack([replica_at, left_at, right_at, far_at]).astype(jnp.int32)
    for start, out in zip(offsets(BACKWARD), outs, strict=True):
        rows = out.shape[2]
        came = lax.all_to_all(
            out.reshape(num_shards, rows, block_size),
            "shard",
            split_axis=0,
            concat_axis=0,
            tiled=True,
        )
        own = from_slots(owners, came)
        from_left, from_right = to_right(own), to_left(own)
        far_left = to_right(from_left[:, : width // 2])
        far_right = to_left(from_right[:, width // 2 :])
        update = place(
            groups,
            (own, from_left, from_right, far_left, far_right),
            start,
            (strip_rows, columns),
            update,
        )
    return (new_left[None], new_right[None], update)


def solution(mesh):
    in_specs = (
        P("replica", "shard", None),
        P(),
        P(("replica", "shard"), None, None, None),
        P(("replica", "shard"), None, None, None),
        P(("replica", "shard"), None, None, None),
        P(("replica", "shard"), None, None, None),
    )
    out_specs = (
        P(("replica", "shard"), None, None, None),
        P(("replica", "shard"), None, None, None),
        P("shard", None),
    )
    return jax.shard_map(body, mesh=mesh, in_specs=in_specs, out_specs=out_specs, check_vma=False)
```

```python
import functools

import jax
import jax.numpy as jnp
from jax import lax
from jax.experimental import pallas as pl
from jax.experimental.pallas import tpu as pltpu
from jax.sharding import PartitionSpec as P

RELAY_FLOPS = 30_000_000_000
BACKWARD = (64,)


def offsets(parts):
    return [sum(parts[:at]) for at in range(len(parts))]


def any_spec():
    return pl.BlockSpec(memory_space=pl.ANY)


def vmem_spec():
    return pl.BlockSpec(memory_space=pltpu.VMEM)


def params(mib=48):
    return pltpu.CompilerParams(vmem_limit_bytes=mib * 1024 * 1024)


def relay_kernel(ahead, passed_right, behind, passed_left, out_right, out_left):
    for mine, passed, out in ((ahead, passed_right, out_right), (behind, passed_left, out_left)):
        out[...] = (mine[...].astype(jnp.float32) + passed[...].astype(jnp.float32)).astype(
            jnp.bfloat16
        )


def relays(ahead, passed_right, behind, passed_left):
    rows, columns = ahead.shape
    return pl.pallas_call(
        relay_kernel,
        out_shape=[jax.ShapeDtypeStruct((rows, columns), jnp.bfloat16)] * 2,
        in_specs=[vmem_spec()] * 4,
        out_specs=[vmem_spec()] * 2,
        compiler_params=params(),
        cost_estimate=pl.CostEstimate(
            flops=RELAY_FLOPS, bytes_accessed=12 * rows * columns, transcendentals=0
        ),
        name="relays",
    )(ahead, passed_right, behind, passed_left)


def slot_kernel(block_size, owners, own, low_a, low_b, high_a, high_b, out, held, sems):
    count, rows = held.shape[:2]
    half = rows // 2
    copies = []
    for at in range(count):
        columns = slice(at * block_size, (at + 1) * block_size)
        for first, one, other in ((0, low_a, low_b), (half, high_a, high_b)):
            total = (
                own[first : first + half, columns].astype(jnp.float32)
                + one[:, columns].astype(jnp.float32)
                + other[:, columns].astype(jnp.float32)
            )
            held[at, first : first + half] = total.astype(jnp.bfloat16)
        copy = pltpu.make_async_copy(held.at[at], out.at[owners[at]], sems.at[at])
        copy.start()
        copies.append(copy)
    for copy in copies:
        copy.wait()


def to_slots(owners, own, lower, upper, num_shards, block_size):
    rows, columns = own.shape
    count = columns // block_size
    return pl.pallas_call(
        functools.partial(slot_kernel, block_size),
        out_shape=jax.ShapeDtypeStruct((num_shards, rows, block_size), jnp.bfloat16),
        in_specs=[pl.BlockSpec(memory_space=pltpu.SMEM)] + [vmem_spec()] * 5,
        out_specs=any_spec(),
        scratch_shapes=[
            pltpu.VMEM((count, rows, block_size), jnp.bfloat16),
            pltpu.SemaphoreType.DMA((count,)),
        ],
        compiler_params=params(),
        cost_estimate=pl.CostEstimate(
            flops=3 * rows * columns, bytes_accessed=8 * rows * columns, transcendentals=0
        ),
        name="to_slots",
    )(owners, own, *lower, *upper)


def whole_block(parts):
    joined = jnp.concatenate([part[0] for part in parts], axis=1)
    return joined.reshape(joined.shape[0] * joined.shape[1], joined.shape[2])


def update_kernel(num_parts, bounds, rows_of, *refs):
    parts = refs[:num_parts]
    left_root, right_root = refs[num_parts], refs[num_parts + 1]
    outs = refs[num_parts + 2 :]
    block = whole_block(parts)
    applied = jnp.dot(left_root[0], block, preferred_element_type=jnp.float32).astype(jnp.bfloat16)
    product = jnp.dot(applied, right_root[0], preferred_element_type=jnp.float32).astype(jnp.bfloat16)
    product = product.reshape(parts[0].shape[1], -1, product.shape[1])
    for out, (start, rows) in zip(outs, bounds, strict=True):
        out[0] = product[:, start : start + rows]


def updates(rows_of, parts, left_roots, right_roots, back):
    capacity, block_size = left_roots.shape[0], left_roots.shape[1]
    block_rows, strips = parts[0].shape[:2]
    bounds = list(zip(offsets(back), back, strict=True))
    at_row = lambda t, rows_of: (rows_of[t], 0, 0, 0)
    root = pl.BlockSpec((1, block_size, block_size), lambda t, rows_of: (t, 0, 0))
    return pl.pallas_call(
        functools.partial(update_kernel, len(parts), bounds),
        grid_spec=pltpu.PrefetchScalarGridSpec(
            num_scalar_prefetch=1,
            grid=(capacity,),
            in_specs=[pl.BlockSpec((1,) + part.shape[1:], at_row) for part in parts] + [root, root],
            out_specs=[pl.BlockSpec((1, strips, rows, block_size), at_row) for rows in back],
        ),
        out_shape=[
            jax.ShapeDtypeStruct((block_rows, strips, rows, block_size), jnp.bfloat16)
            for rows in back
        ],
        compiler_params=params(),
        cost_estimate=pl.CostEstimate(
            flops=4 * capacity * block_size**3,
            bytes_accessed=8 * capacity * block_size**2,
            transcendentals=0,
        ),
        name="updates",
    )(rows_of, *parts, left_roots, right_roots)


def gram_kernel(num_parts, rows_of, named, *refs):
    parts = refs[:num_parts]
    left, right, new_left, new_right = refs[num_parts:]
    block = whole_block(parts)
    size = block.shape[0]
    holds = named[pl.program_id(0)] > 0
    scale = 0.1 / size
    gram = lax.dot_general(block, block, (((1,), (1,)), ((), ())), preferred_element_type=jnp.float32)
    new_left[0] = 0.9 * left[0] + jnp.where(holds, scale * gram, 0.0)
    gram = lax.dot_general(block, block, (((0,), (0,)), ((), ())), preferred_element_type=jnp.float32)
    new_right[0] = 0.9 * right[0] + jnp.where(holds, scale * gram, 0.0)


def statistics(rows_of, named, parts, factor_left, factor_right):
    capacity, block_size = factor_left.shape[0], factor_left.shape[1]
    at_row = lambda t, rows_of, named: (rows_of[t], 0, 0, 0)
    square = pl.BlockSpec((1, block_size, block_size), lambda t, rows_of, named: (t, 0, 0))
    return pl.pallas_call(
        functools.partial(gram_kernel, len(parts)),
        grid_spec=pltpu.PrefetchScalarGridSpec(
            num_scalar_prefetch=2,
            grid=(capacity,),
            in_specs=[pl.BlockSpec((1,) + part.shape[1:], at_row) for part in parts]
            + [square, square],
            out_specs=[square, square],
        ),
        out_shape=[jax.ShapeDtypeStruct(factor_left.shape, jnp.float32)] * 2,
        compiler_params=params(),
        cost_estimate=pl.CostEstimate(
            flops=4 * capacity * block_size**3,
            bytes_accessed=18 * capacity * block_size**2,
            transcendentals=0,
        ),
        name="statistics",
    )(rows_of, named, *parts, factor_left, factor_right)


def pick_kernel(block_size, count, owners, slots, low, high, sems):
    copies = []
    for at in range(2 * count):
        out, first = (low, at) if at < count else (high, at - count)
        columns = pl.ds(first * block_size, block_size)
        copy = pltpu.make_async_copy(slots.at[owners[at]], out.at[:, columns], sems.at[at])
        copy.start()
        copies.append(copy)
    for copy in copies:
        copy.wait()


def from_slots(owners, slots):
    count = owners.shape[0] // 2
    _, rows, block_size = slots.shape
    return pl.pallas_call(
        functools.partial(pick_kernel, block_size, count),
        out_shape=[jax.ShapeDtypeStruct((rows, count * block_size), jnp.bfloat16)] * 2,
        in_specs=[pl.BlockSpec(memory_space=pltpu.SMEM), any_spec()],
        out_specs=[vmem_spec()] * 2,
        scratch_shapes=[pltpu.SemaphoreType.DMA((2 * count,))],
        compiler_params=params(),
        cost_estimate=pl.CostEstimate(
            flops=0, bytes_accessed=8 * rows * count * block_size, transcendentals=0
        ),
        name="from_slots",
    )(owners, slots)


def place_kernel(groups, *refs):
    pieces, out, sems = refs[:-2], refs[-2], refs[-1]
    half = pieces[0].shape[1]
    copies = []
    for at, piece in enumerate(pieces):
        first = pl.multiple_of(groups[at // 2] * (2 * half) + at % 2 * half, 128)
        copy = pltpu.make_async_copy(piece, out.at[:, pl.ds(first, half)], sems.at[at])
        copy.start()
        copies.append(copy)
    for copy in copies:
        copy.wait()


def place(groups, pieces, shape):
    return pl.pallas_call(
        place_kernel,
        out_shape=jax.ShapeDtypeStruct(shape, jnp.bfloat16),
        in_specs=[pl.BlockSpec(memory_space=pltpu.SMEM)] + [vmem_spec()] * len(pieces),
        out_specs=any_spec(),
        scratch_shapes=[pltpu.SemaphoreType.DMA((len(pieces),))],
        compiler_params=params(),
        cost_estimate=pl.CostEstimate(
            flops=0, bytes_accessed=4 * shape[0] * shape[1], transcendentals=0
        ),
        name="place",
    )(groups, *pieces)


def body(grads, owner_map, factor_left, factor_right, left_inverse_roots, right_inverse_roots):
    num_replicas = lax.axis_size("replica")
    num_shards = lax.axis_size("shard")
    replica_at = lax.axis_index("replica")
    shard_at = lax.axis_index("shard")
    strip_rows, columns = grads.shape[1], grads.shape[2]
    capacity, block_size = factor_left.shape[1], factor_left.shape[2]
    block_rows, block_cols = owner_map.shape
    per_group = block_cols // num_replicas
    width = per_group * block_size
    strips = block_size // strip_rows
    onward = [(at, (at + 1) % num_replicas) for at in range(num_replicas)]
    back = [(at, (at - 1) % num_replicas) for at in range(num_replicas)]
    to_right = lambda a: lax.ppermute(a, "replica", onward)
    to_left = lambda a: lax.ppermute(a, "replica", back)
    right_at = (replica_at + 1) % num_replicas
    left_at = (replica_at + num_replicas - 1) % num_replicas
    far_at = (replica_at + 2) % num_replicas

    group_entries = lax.dynamic_slice_in_dim(owner_map, replica_at * per_group, per_group, 1)
    row_entries = lax.dynamic_index_in_dim(group_entries, shard_at // strips, 0, keepdims=False)
    owners = row_entries // capacity
    targets = shard_at * capacity + jnp.arange(capacity, dtype=jnp.int32)
    match = jnp.any(group_entries[None] == targets[:, None, None], axis=2)
    named = jnp.any(match, axis=1)
    unused = jnp.logical_not(jnp.any(match, axis=0))
    rank_slot = jnp.cumsum(jnp.logical_not(named).astype(jnp.int32))
    rank_row = jnp.cumsum(unused.astype(jnp.int32))
    spare = jnp.logical_and(
        jnp.logical_and(jnp.logical_not(named)[:, None], unused[None]),
        rank_slot[:, None] == rank_row[None],
    )
    chosen = jnp.logical_or(match, spare)
    rows_of = jnp.sum(
        jnp.where(chosen, jnp.arange(block_rows, dtype=jnp.int32)[None], 0), axis=1
    ).astype(jnp.int32)
    named = named.astype(jnp.int32)

    tile = 8
    view = grads[0].reshape(strip_rows // tile, tile, num_replicas, width).transpose(0, 2, 1, 3)

    def piece(group, start, rows):
        part = lax.dynamic_slice(
            view, (start // tile, group, 0, 0), (rows // tile, 1, tile, width)
        )
        return part.reshape(rows, width)

    half = strip_rows // 2
    far = (piece(far_at, 0, half), piece(far_at, half, half))
    (ahead_at, behind_at), far = lax.optimization_barrier(((right_at, left_at), far))
    passed_right, passed_left = to_right(far[0]), to_left(far[1])
    plain_right = to_right(piece(ahead_at, half, half))
    plain_left = to_left(piece(behind_at, 0, half))
    ahead, behind = relays(
        piece(right_at, 0, half), passed_right, piece(left_at, half, half), passed_left
    )
    added_right, added_left = to_right(ahead), to_left(behind)
    lower = (plain_left, added_right)
    upper = (added_left, plain_right)
    groups = jnp.stack([replica_at, left_at, right_at, far_at]).astype(jnp.int32)
    upper, rows_of, named, groups = lax.optimization_barrier((upper, rows_of, named, groups))
    own = piece(replica_at, 0, strip_rows)
    slots = to_slots(owners, own, lower, upper, num_shards, block_size)
    came = lax.all_to_all(slots, "shard", split_axis=0, concat_axis=0, tiled=True)
    arrived = [came.reshape(block_rows, strips, strip_rows, block_size)]

    outs = updates(rows_of, arrived, left_inverse_roots[0], right_inverse_roots[0], BACKWARD)
    new_left, new_right = statistics(rows_of, named, arrived, factor_left[0], factor_right[0])

    returned = lax.all_to_all(
        outs[0].reshape(num_shards, strip_rows, block_size),
        "shard",
        split_axis=0,
        concat_axis=0,
        tiled=True,
    )
    low, high = from_slots(owners, returned)
    later, (low, high) = lax.optimization_barrier((owners, (low, high)))
    left_low, right_high = to_right(low), to_left(high)
    own_low, own_high = from_slots(later, returned)
    left_high, right_low = to_right(own_high), to_left(own_low)
    far_low, far_high = to_right(left_low), to_left(right_high)
    update = place(
        groups,
        (own_low, own_high, left_low, left_high, right_low, right_high, far_low, far_high),
        (strip_rows, columns),
    )
    return (new_left[None], new_right[None], update)


def solution(mesh):
    in_specs = (
        P("replica", "shard", None),
        P(),
        P(("replica", "shard"), None, None, None),
        P(("replica", "shard"), None, None, None),
        P(("replica", "shard"), None, None, None),
        P(("replica", "shard"), None, None, None),
    )
    out_specs = (
        P(("replica", "shard"), None, None, None),
        P(("replica", "shard"), None, None, None),
        P("shard", None),
    )
    return jax.shard_map(body, mesh=mesh, in_specs=in_specs, out_specs=out_specs, check_vma=False)
```

```python
import functools

import jax
import jax.numpy as jnp
from jax import lax
from jax.experimental import pallas as pl
from jax.experimental.pallas import tpu as pltpu
from jax.sharding import PartitionSpec as P

RELAY_FLOPS = 30_000_000_000


def any_spec():
    return pl.BlockSpec(memory_space=pl.ANY)


def vmem_spec():
    return pl.BlockSpec(memory_space=pltpu.VMEM)


def params(mib=48):
    return pltpu.CompilerParams(vmem_limit_bytes=mib * 1024 * 1024)


def relay_kernel(ahead, passed_right, behind, passed_left, out_right, out_left):
    for mine, passed, out in ((ahead, passed_right, out_right), (behind, passed_left, out_left)):
        out[...] = (mine[...].astype(jnp.float32) + passed[...].astype(jnp.float32)).astype(
            jnp.bfloat16
        )


def relays(ahead, passed_right, behind, passed_left):
    rows, columns = ahead.shape
    return pl.pallas_call(
        relay_kernel,
        out_shape=[jax.ShapeDtypeStruct((rows, columns), jnp.bfloat16)] * 2,
        in_specs=[vmem_spec()] * 4,
        out_specs=[vmem_spec()] * 2,
        compiler_params=params(),
        cost_estimate=pl.CostEstimate(
            flops=RELAY_FLOPS, bytes_accessed=12 * rows * columns, transcendentals=0
        ),
        name="relays",
    )(ahead, passed_right, behind, passed_left)


def slot_kernel(block_size, owners, own, low_a, low_b, high_a, high_b, out):
    half = own.shape[0] // 2
    for at in range(own.shape[1] // block_size):
        columns = slice(at * block_size, (at + 1) * block_size)
        for first, one, other in ((0, low_a, low_b), (half, high_a, high_b)):
            total = (
                own[first : first + half, columns].astype(jnp.float32)
                + one[:, columns].astype(jnp.float32)
                + other[:, columns].astype(jnp.float32)
            )
            out[owners[at], first : first + half] = total.astype(jnp.bfloat16)


def to_slots(owners, own, lower, upper, num_shards, block_size):
    rows, columns = own.shape
    return pl.pallas_call(
        functools.partial(slot_kernel, block_size),
        out_shape=jax.ShapeDtypeStruct((num_shards, rows, block_size), jnp.bfloat16),
        in_specs=[pl.BlockSpec(memory_space=pltpu.SMEM)] + [vmem_spec()] * 5,
        out_specs=vmem_spec(),
        compiler_params=params(),
        cost_estimate=pl.CostEstimate(
            flops=3 * rows * columns, bytes_accessed=8 * rows * columns, transcendentals=0
        ),
        name="to_slots",
    )(owners, own, *lower, *upper)


def update_kernel(rows_of, blocks, left_roots, right_roots, out):
    for slot in range(left_roots.shape[0]):
        block = blocks[rows_of[slot]]
        applied = jnp.dot(left_roots[slot], block, preferred_element_type=jnp.float32)
        product = jnp.dot(
            applied.astype(jnp.bfloat16), right_roots[slot], preferred_element_type=jnp.float32
        )
        out[rows_of[slot]] = product.astype(jnp.bfloat16)


def updates(rows_of, blocks, left_roots, right_roots):
    capacity, block_size = left_roots.shape[0], left_roots.shape[1]
    return pl.pallas_call(
        update_kernel,
        out_shape=jax.ShapeDtypeStruct(blocks.shape, jnp.bfloat16),
        in_specs=[pl.BlockSpec(memory_space=pltpu.SMEM)] + [vmem_spec()] * 3,
        out_specs=vmem_spec(),
        compiler_params=params(),
        cost_estimate=pl.CostEstimate(
            flops=4 * capacity * block_size**3,
            bytes_accessed=8 * capacity * block_size**2,
            transcendentals=0,
        ),
        name="updates",
    )(rows_of, blocks, left_roots, right_roots)


def gram_kernel(rows_of, named, blocks, left, right, new_left, new_right):
    block = blocks[0]
    holds = named[pl.program_id(0)] > 0
    scale = 0.1 / block.shape[0]
    gram = lax.dot_general(block, block, (((1,), (1,)), ((), ())), preferred_element_type=jnp.float32)
    new_left[0] = 0.9 * left[0] + jnp.where(holds, scale * gram, 0.0)
    gram = lax.dot_general(block, block, (((0,), (0,)), ((), ())), preferred_element_type=jnp.float32)
    new_right[0] = 0.9 * right[0] + jnp.where(holds, scale * gram, 0.0)


def statistics(rows_of, named, blocks, factor_left, factor_right):
    capacity, block_size = factor_left.shape[0], factor_left.shape[1]
    at_row = lambda t, rows_of, named: (rows_of[t], 0, 0)
    square = pl.BlockSpec((1, block_size, block_size), lambda t, rows_of, named: (t, 0, 0))
    return pl.pallas_call(
        gram_kernel,
        grid_spec=pltpu.PrefetchScalarGridSpec(
            num_scalar_prefetch=2,
            grid=(capacity,),
            in_specs=[pl.BlockSpec((1, block_size, block_size), at_row), square, square],
            out_specs=[square, square],
        ),
        out_shape=[jax.ShapeDtypeStruct(factor_left.shape, jnp.float32)] * 2,
        compiler_params=params(),
        cost_estimate=pl.CostEstimate(
            flops=4 * capacity * block_size**3,
            bytes_accessed=18 * capacity * block_size**2,
            transcendentals=0,
        ),
        name="statistics",
    )(rows_of, named, blocks, factor_left, factor_right)


def pick_kernel(block_size, owners, slots, low, high):
    count = low.shape[1] // block_size
    for at in range(2 * count):
        out, first = (low, at) if at < count else (high, at - count)
        out[:, first * block_size : (first + 1) * block_size] = slots[owners[at]]


def from_slots(owners, slots):
    count = owners.shape[0] // 2
    _, rows, block_size = slots.shape
    return pl.pallas_call(
        functools.partial(pick_kernel, block_size),
        out_shape=[jax.ShapeDtypeStruct((rows, count * block_size), jnp.bfloat16)] * 2,
        in_specs=[pl.BlockSpec(memory_space=pltpu.SMEM), vmem_spec()],
        out_specs=[vmem_spec()] * 2,
        compiler_params=params(),
        cost_estimate=pl.CostEstimate(
            flops=0, bytes_accessed=8 * rows * count * block_size, transcendentals=0
        ),
        name="from_slots",
    )(owners, slots)


def place_kernel(groups, *refs):
    pieces, out, sems = refs[: 2 * groups.shape[0]], refs[-2], refs[-1]
    half = pieces[0].shape[1]
    copies = []
    for at, piece in enumerate(pieces):
        first = pl.multiple_of(groups[at // 2] * (2 * half) + at % 2 * half, 128)
        copy = pltpu.make_async_copy(piece, out.at[:, pl.ds(first, half)], sems.at[at])
        copy.start()
        copies.append(copy)
    for copy in copies:
        copy.wait()


def place(groups, pieces, shape, held=()):
    return pl.pallas_call(
        place_kernel,
        out_shape=jax.ShapeDtypeStruct(shape, jnp.bfloat16),
        in_specs=[pl.BlockSpec(memory_space=pltpu.SMEM)]
        + [vmem_spec()] * len(pieces)
        + [any_spec()] * len(held),
        out_specs=any_spec(),
        scratch_shapes=[pltpu.SemaphoreType.DMA((len(pieces),))],
        input_output_aliases={1 + len(pieces): 0} if held else {},
        compiler_params=params(),
        cost_estimate=pl.CostEstimate(
            flops=0,
            bytes_accessed=4 * len(pieces) * pieces[0].shape[0] * pieces[0].shape[1],
            transcendentals=0,
        ),
        name="place",
    )(groups, *pieces, *held)


def body(grads, owner_map, factor_left, factor_right, left_inverse_roots, right_inverse_roots):
    num_replicas = lax.axis_size("replica")
    num_shards = lax.axis_size("shard")
    replica_at = lax.axis_index("replica")
    shard_at = lax.axis_index("shard")
    strip_rows, columns = grads.shape[1], grads.shape[2]
    capacity, block_size = factor_left.shape[1], factor_left.shape[2]
    block_rows, block_cols = owner_map.shape
    per_group = block_cols // num_replicas
    width = per_group * block_size
    strips = block_size // strip_rows
    onward = [(at, (at + 1) % num_replicas) for at in range(num_replicas)]
    back = [(at, (at - 1) % num_replicas) for at in range(num_replicas)]
    to_right = lambda a: lax.ppermute(a, "replica", onward)
    to_left = lambda a: lax.ppermute(a, "replica", back)
    right_at = (replica_at + 1) % num_replicas
    left_at = (replica_at + num_replicas - 1) % num_replicas
    far_at = (replica_at + 2) % num_replicas

    group_entries = lax.dynamic_slice_in_dim(owner_map, replica_at * per_group, per_group, 1)
    row_entries = lax.dynamic_index_in_dim(group_entries, shard_at // strips, 0, keepdims=False)
    owners = row_entries // capacity
    targets = shard_at * capacity + jnp.arange(capacity, dtype=jnp.int32)
    match = jnp.any(group_entries[None] == targets[:, None, None], axis=2)
    named = jnp.any(match, axis=1)
    unused = jnp.logical_not(jnp.any(match, axis=0))
    rank_slot = jnp.cumsum(jnp.logical_not(named).astype(jnp.int32))
    rank_row = jnp.cumsum(unused.astype(jnp.int32))
    spare = jnp.logical_and(
        jnp.logical_and(jnp.logical_not(named)[:, None], unused[None]),
        rank_slot[:, None] == rank_row[None],
    )
    chosen = jnp.logical_or(match, spare)
    rows_of = jnp.sum(
        jnp.where(chosen, jnp.arange(block_rows, dtype=jnp.int32)[None], 0), axis=1
    ).astype(jnp.int32)
    named = named.astype(jnp.int32)

    tile = 8
    view = grads[0].reshape(strip_rows // tile, tile, num_replicas, width).transpose(0, 2, 1, 3)

    def piece(group, start, rows):
        part = lax.dynamic_slice(
            view, (start // tile, group, 0, 0), (rows // tile, 1, tile, width)
        )
        return part.reshape(rows, width)

    half = strip_rows // 2
    far = (piece(far_at, 0, half), piece(far_at, half, half))
    (ahead_at, behind_at), far = lax.optimization_barrier(((right_at, left_at), far))
    passed_right, passed_left = to_right(far[0]), to_left(far[1])
    plain_right = to_right(piece(ahead_at, half, half))
    plain_left = to_left(piece(behind_at, 0, half))
    ahead, behind = relays(
        piece(right_at, 0, half), passed_right, piece(left_at, half, half), passed_left
    )
    added_right, added_left = to_right(ahead), to_left(behind)
    lower = (plain_left, added_right)
    upper = (added_left, plain_right)
    groups = jnp.stack([replica_at, left_at, right_at, far_at]).astype(jnp.int32)
    upper, rows_of, named, groups = lax.optimization_barrier((upper, rows_of, named, groups))
    own = piece(replica_at, 0, strip_rows)
    slots = to_slots(owners, own, lower, upper, num_shards, block_size)
    came = lax.all_to_all(slots, "shard", split_axis=0, concat_axis=0, tiled=True)
    blocks = came.reshape(block_rows, block_size, block_size)
    outs = updates(rows_of, blocks, left_inverse_roots[0], right_inverse_roots[0])
    new_left, new_right = statistics(rows_of, named, blocks, factor_left[0], factor_right[0])

    returned = lax.all_to_all(
        outs.reshape(num_shards, strip_rows, block_size),
        "shard",
        split_axis=0,
        concat_axis=0,
        tiled=True,
    )
    low, high = from_slots(owners, returned)
    later, (low, high) = lax.optimization_barrier((owners, (low, high)))
    left_low, right_high = to_right(low), to_left(high)
    own_low, own_high = from_slots(later, returned)
    left_high, right_low = to_right(own_high), to_left(own_low)
    far_low, far_high = to_right(left_low), to_left(right_high)
    near = (own_low, own_high, left_low, left_high, right_low, right_high)
    update = place(groups[:3], near, (strip_rows, columns))
    update = place(groups[3:], (far_low, far_high), (strip_rows, columns), (update,))
    return (new_left[None], new_right[None], update)


def solution(mesh):
    in_specs = (
        P("replica", "shard", None),
        P(),
        P(("replica", "shard"), None, None, None),
        P(("replica", "shard"), None, None, None),
        P(("replica", "shard"), None, None, None),
        P(("replica", "shard"), None, None, None),
    )
    out_specs = (
        P(("replica", "shard"), None, None, None),
        P(("replica", "shard"), None, None, None),
        P("shard", None),
    )
    return jax.shard_map(body, mesh=mesh, in_specs=in_specs, out_specs=out_specs, check_vma=False)
```

```python
import functools

import jax
import jax.numpy as jnp
from jax import lax
from jax.experimental import pallas as pl
from jax.experimental.pallas import tpu as pltpu
from jax.sharding import PartitionSpec as P

RELAY_FLOPS = 30_000_000_000


def any_spec():
    return pl.BlockSpec(memory_space=pl.ANY)


def vmem_spec():
    return pl.BlockSpec(memory_space=pltpu.VMEM)


def params(mib=16):
    return pltpu.CompilerParams(vmem_limit_bytes=mib * 1024 * 1024)


def relay_kernel(ahead, passed_right, behind, passed_left, out_right, out_left):
    for mine, passed, out in ((ahead, passed_right, out_right), (behind, passed_left, out_left)):
        out[...] = (mine[...].astype(jnp.float32) + passed[...].astype(jnp.float32)).astype(
            jnp.bfloat16
        )


def relays(ahead, passed_right, behind, passed_left):
    rows, columns = ahead.shape
    return pl.pallas_call(
        relay_kernel,
        out_shape=[jax.ShapeDtypeStruct((rows, columns), jnp.bfloat16)] * 2,
        in_specs=[vmem_spec()] * 4,
        out_specs=[vmem_spec()] * 2,
        compiler_params=params(),
        cost_estimate=pl.CostEstimate(
            flops=RELAY_FLOPS, bytes_accessed=12 * rows * columns, transcendentals=0
        ),
        name="relays",
    )(ahead, passed_right, behind, passed_left)


def slot_kernel(block_size, owners, own, low_a, low_b, high_a, high_b, out):
    half = own.shape[0] // 2
    for at in range(own.shape[1] // block_size):
        columns = slice(at * block_size, (at + 1) * block_size)
        for first, one, other in ((0, low_a, low_b), (half, high_a, high_b)):
            total = (
                own[first : first + half, columns].astype(jnp.float32)
                + one[:, columns].astype(jnp.float32)
                + other[:, columns].astype(jnp.float32)
            )
            out[owners[at], first : first + half] = total.astype(jnp.bfloat16)


def to_slots(owners, own, lower, upper, num_shards, block_size):
    rows, columns = own.shape
    return pl.pallas_call(
        functools.partial(slot_kernel, block_size),
        out_shape=jax.ShapeDtypeStruct((num_shards, rows, block_size), jnp.bfloat16),
        in_specs=[pl.BlockSpec(memory_space=pltpu.SMEM)] + [vmem_spec()] * 5,
        out_specs=vmem_spec(),
        compiler_params=params(),
        cost_estimate=pl.CostEstimate(
            flops=3 * rows * columns, bytes_accessed=8 * rows * columns, transcendentals=0
        ),
        name="to_slots",
    )(owners, own, *lower, *upper)


def update_kernel(rows_of, blocks, left_roots, right_roots, out):
    for slot in range(left_roots.shape[0]):
        block = blocks[rows_of[slot]]
        applied = jnp.dot(left_roots[slot], block, preferred_element_type=jnp.float32)
        product = jnp.dot(
            applied.astype(jnp.bfloat16), right_roots[slot], preferred_element_type=jnp.float32
        )
        out[rows_of[slot]] = product.astype(jnp.bfloat16)


def updates(rows_of, blocks, left_roots, right_roots):
    capacity, block_size = left_roots.shape[0], left_roots.shape[1]
    return pl.pallas_call(
        update_kernel,
        out_shape=jax.ShapeDtypeStruct(blocks.shape, jnp.bfloat16),
        in_specs=[pl.BlockSpec(memory_space=pltpu.SMEM)] + [vmem_spec()] * 3,
        out_specs=vmem_spec(),
        compiler_params=params(),
        cost_estimate=pl.CostEstimate(
            flops=4 * capacity * block_size**3,
            bytes_accessed=8 * capacity * block_size**2,
            transcendentals=0,
        ),
        name="updates",
    )(rows_of, blocks, left_roots, right_roots)


def gram_kernel(rows_of, named, blocks, left, right, new_left, new_right):
    block = blocks[0]
    holds = named[pl.program_id(0)] > 0
    scale = 0.1 / block.shape[0]
    gram = lax.dot_general(block, block, (((1,), (1,)), ((), ())), preferred_element_type=jnp.float32)
    new_left[0] = 0.9 * left[0] + jnp.where(holds, scale * gram, 0.0)
    gram = lax.dot_general(block, block, (((0,), (0,)), ((), ())), preferred_element_type=jnp.float32)
    new_right[0] = 0.9 * right[0] + jnp.where(holds, scale * gram, 0.0)


def statistics(rows_of, named, blocks, factor_left, factor_right):
    capacity, block_size = factor_left.shape[0], factor_left.shape[1]
    at_row = lambda t, rows_of, named: (rows_of[t], 0, 0)
    square = pl.BlockSpec((1, block_size, block_size), lambda t, rows_of, named: (t, 0, 0))
    return pl.pallas_call(
        gram_kernel,
        grid_spec=pltpu.PrefetchScalarGridSpec(
            num_scalar_prefetch=2,
            grid=(capacity,),
            in_specs=[pl.BlockSpec((1, block_size, block_size), at_row), square, square],
            out_specs=[square, square],
        ),
        out_shape=[jax.ShapeDtypeStruct(factor_left.shape, jnp.float32)] * 2,
        compiler_params=params(),
        cost_estimate=pl.CostEstimate(
            flops=4 * capacity * block_size**3,
            bytes_accessed=18 * capacity * block_size**2,
            transcendentals=0,
        ),
        name="statistics",
    )(rows_of, named, blocks, factor_left, factor_right)


def pick_kernel(block_size, owners, slots, low, high):
    count = low.shape[1] // block_size
    for at in range(2 * count):
        out, first = (low, at) if at < count else (high, at - count)
        out[:, first * block_size : (first + 1) * block_size] = slots[owners[at]]


def from_slots(owners, slots):
    count = owners.shape[0] // 2
    _, rows, block_size = slots.shape
    return pl.pallas_call(
        functools.partial(pick_kernel, block_size),
        out_shape=[jax.ShapeDtypeStruct((rows, count * block_size), jnp.bfloat16)] * 2,
        in_specs=[pl.BlockSpec(memory_space=pltpu.SMEM), vmem_spec()],
        out_specs=[vmem_spec()] * 2,
        compiler_params=params(),
        cost_estimate=pl.CostEstimate(
            flops=0, bytes_accessed=8 * rows * count * block_size, transcendentals=0
        ),
        name="from_slots",
    )(owners, slots)


def place_kernel(groups, *refs):
    pieces, out, sems = refs[: 2 * groups.shape[0]], refs[-2], refs[-1]
    half = pieces[0].shape[1]
    copies = []
    for at, piece in enumerate(pieces):
        first = pl.multiple_of(groups[at // 2] * (2 * half) + at % 2 * half, 128)
        copy = pltpu.make_async_copy(piece, out.at[:, pl.ds(first, half)], sems.at[at])
        copy.start()
        copies.append(copy)
    for copy in copies:
        copy.wait()


def place(groups, pieces, shape, held=()):
    return pl.pallas_call(
        place_kernel,
        out_shape=jax.ShapeDtypeStruct(shape, jnp.bfloat16),
        in_specs=[pl.BlockSpec(memory_space=pltpu.SMEM)]
        + [vmem_spec()] * len(pieces)
        + [any_spec()] * len(held),
        out_specs=any_spec(),
        scratch_shapes=[pltpu.SemaphoreType.DMA((len(pieces),))],
        input_output_aliases={1 + len(pieces): 0} if held else {},
        compiler_params=params(),
        cost_estimate=pl.CostEstimate(
            flops=0,
            bytes_accessed=4 * len(pieces) * pieces[0].shape[0] * pieces[0].shape[1],
            transcendentals=0,
        ),
        name="place",
    )(groups, *pieces, *held)


def body(grads, owner_map, factor_left, factor_right, left_inverse_roots, right_inverse_roots):
    num_replicas = lax.axis_size("replica")
    num_shards = lax.axis_size("shard")
    replica_at = lax.axis_index("replica")
    shard_at = lax.axis_index("shard")
    strip_rows, columns = grads.shape[1], grads.shape[2]
    capacity, block_size = factor_left.shape[1], factor_left.shape[2]
    block_rows, block_cols = owner_map.shape
    per_group = block_cols // num_replicas
    width = per_group * block_size
    strips = block_size // strip_rows
    onward = [(at, (at + 1) % num_replicas) for at in range(num_replicas)]
    back = [(at, (at - 1) % num_replicas) for at in range(num_replicas)]
    to_right = lambda a: lax.ppermute(a, "replica", onward)
    to_left = lambda a: lax.ppermute(a, "replica", back)
    right_at = (replica_at + 1) % num_replicas
    left_at = (replica_at + num_replicas - 1) % num_replicas
    far_at = (replica_at + 2) % num_replicas

    group_entries = lax.dynamic_slice_in_dim(owner_map, replica_at * per_group, per_group, 1)
    row_entries = lax.dynamic_index_in_dim(group_entries, shard_at // strips, 0, keepdims=False)
    owners = row_entries // capacity
    targets = shard_at * capacity + jnp.arange(capacity, dtype=jnp.int32)
    match = jnp.any(group_entries[None] == targets[:, None, None], axis=2)
    named = jnp.any(match, axis=1)
    unused = jnp.logical_not(jnp.any(match, axis=0))
    rank_slot = jnp.cumsum(jnp.logical_not(named).astype(jnp.int32))
    rank_row = jnp.cumsum(unused.astype(jnp.int32))
    spare = jnp.logical_and(
        jnp.logical_and(jnp.logical_not(named)[:, None], unused[None]),
        rank_slot[:, None] == rank_row[None],
    )
    chosen = jnp.logical_or(match, spare)
    rows_of = jnp.sum(
        jnp.where(chosen, jnp.arange(block_rows, dtype=jnp.int32)[None], 0), axis=1
    ).astype(jnp.int32)
    named = named.astype(jnp.int32)

    tile = 8
    view = grads[0].reshape(strip_rows // tile, tile, num_replicas, width).transpose(0, 2, 1, 3)

    def piece(group, start, rows):
        part = lax.dynamic_slice(
            view, (start // tile, group, 0, 0), (rows // tile, 1, tile, width)
        )
        return part.reshape(rows, width)

    half = strip_rows // 2
    far = (piece(far_at, 0, half), piece(far_at, half, half))
    (ahead_at, behind_at), far = lax.optimization_barrier(((right_at, left_at), far))
    passed_right, passed_left = to_right(far[0]), to_left(far[1])
    plain_right = to_right(piece(ahead_at, half, half))
    plain_left = to_left(piece(behind_at, 0, half))
    ahead, behind = relays(
        piece(right_at, 0, half), passed_right, piece(left_at, half, half), passed_left
    )
    added_right, added_left = to_right(ahead), to_left(behind)
    lower = (plain_left, added_right)
    upper = (added_left, plain_right)
    groups = jnp.stack([replica_at, left_at, right_at, far_at]).astype(jnp.int32)
    upper, rows_of, named, groups = lax.optimization_barrier((upper, rows_of, named, groups))
    own = piece(replica_at, 0, strip_rows)
    slots = to_slots(owners, own, lower, upper, num_shards, block_size)
    came = lax.all_to_all(slots, "shard", split_axis=0, concat_axis=0, tiled=True)
    blocks = came.reshape(block_rows, block_size, block_size)
    outs = updates(rows_of, blocks, left_inverse_roots[0], right_inverse_roots[0])
    new_left, new_right = statistics(rows_of, named, blocks, factor_left[0], factor_right[0])

    returned = lax.all_to_all(
        outs.reshape(num_shards, strip_rows, block_size),
        "shard",
        split_axis=0,
        concat_axis=0,
        tiled=True,
    )
    low, high = from_slots(owners, returned)
    later, (low, high) = lax.optimization_barrier((owners, (low, high)))
    left_low, right_high = to_right(low), to_left(high)
    own_low, own_high = from_slots(later, returned)
    left_high, right_low = to_right(own_high), to_left(own_low)
    far_low, far_high = to_right(left_low), to_left(right_high)
    near = (own_low, own_high, left_low, left_high, right_low, right_high)
    update = place(groups[:3], near, (strip_rows, columns))
    update = place(groups[3:], (far_low, far_high), (strip_rows, columns), (update,))
    return (new_left[None], new_right[None], update)


def solution(mesh):
    in_specs = (
        P("replica", "shard", None),
        P(),
        P(("replica", "shard"), None, None, None),
        P(("replica", "shard"), None, None, None),
        P(("replica", "shard"), None, None, None),
        P(("replica", "shard"), None, None, None),
    )
    out_specs = (
        P(("replica", "shard"), None, None, None),
        P(("replica", "shard"), None, None, None),
        P("shard", None),
    )
    return jax.shard_map(body, mesh=mesh, in_specs=in_specs, out_specs=out_specs, check_vma=False)
```

```python
import functools

import jax
import jax.numpy as jnp
from jax import lax
from jax.experimental import pallas as pl
from jax.experimental.pallas import tpu as pltpu
from jax.sharding import PartitionSpec as P

AHEAD = 30_000_000_000
BACKWARD = (48, 16)


def any_spec():
    return pl.BlockSpec(memory_space=pl.ANY)


def vmem_spec():
    return pl.BlockSpec(memory_space=pltpu.VMEM)


def params(mib=16):
    return pltpu.CompilerParams(vmem_limit_bytes=mib * 1024 * 1024)


def cut_kernel(cuts, groups, grads, *refs):
    outs, sems = refs[-1 - len(cuts) : -1], refs[-1]
    width = outs[0].shape[1]
    copies = []
    for at, (out, (group, start)) in enumerate(zip(outs, cuts, strict=True)):
        first = pl.multiple_of(groups[group] * width, 128)
        part = grads.at[0, pl.ds(start, out.shape[0]), pl.ds(first, width)]
        copy = pltpu.make_async_copy(part, out, sems.at[at])
        copy.start()
        copies.append(copy)
    for copy in copies:
        copy.wait()


def cut(groups, grads, cuts, width, after=()):
    total = sum(rows for _, _, rows in cuts) * width
    return pl.pallas_call(
        functools.partial(cut_kernel, [(group, start) for group, start, _ in cuts]),
        out_shape=[jax.ShapeDtypeStruct((rows, width), jnp.bfloat16) for _, _, rows in cuts],
        in_specs=[pl.BlockSpec(memory_space=pltpu.SMEM), pl.BlockSpec(memory_space=pltpu.HBM)]
        + [any_spec()] * len(after),
        out_specs=[vmem_spec()] * len(cuts),
        scratch_shapes=[pltpu.SemaphoreType.DMA((len(cuts),))],
        compiler_params=params(),
        cost_estimate=pl.CostEstimate(flops=0, bytes_accessed=4 * total, transcendentals=0),
        name="cut",
    )(groups, pltpu.with_memory_space_constraint(grads, pltpu.HBM), *after)


def relay_kernel(ahead, passed_right, behind, passed_left, out_right, out_left):
    for mine, passed, out in ((ahead, passed_right, out_right), (behind, passed_left, out_left)):
        out[...] = (mine[...].astype(jnp.float32) + passed[...].astype(jnp.float32)).astype(
            jnp.bfloat16
        )


def relays(ahead, passed_right, behind, passed_left):
    rows, columns = ahead.shape
    return pl.pallas_call(
        relay_kernel,
        out_shape=[jax.ShapeDtypeStruct((rows, columns), jnp.bfloat16)] * 2,
        in_specs=[vmem_spec()] * 4,
        out_specs=[vmem_spec()] * 2,
        compiler_params=params(),
        cost_estimate=pl.CostEstimate(
            flops=AHEAD, bytes_accessed=12 * rows * columns, transcendentals=0
        ),
        name="relays",
    )(ahead, passed_right, behind, passed_left)


def slot_kernel(block_size, owners, own, low_a, low_b, high_a, high_b, out):
    half = own.shape[0] // 2
    for at in range(own.shape[1] // block_size):
        columns = slice(at * block_size, (at + 1) * block_size)
        for first, one, other in ((0, low_a, low_b), (half, high_a, high_b)):
            total = (
                own[first : first + half, columns].astype(jnp.float32)
                + one[:, columns].astype(jnp.float32)
                + other[:, columns].astype(jnp.float32)
            )
            out[owners[at], first : first + half] = total.astype(jnp.bfloat16)


def to_slots(owners, own, lower, upper, num_shards, block_size):
    rows, columns = own.shape
    return pl.pallas_call(
        functools.partial(slot_kernel, block_size),
        out_shape=jax.ShapeDtypeStruct((num_shards, rows, block_size), jnp.bfloat16),
        in_specs=[pl.BlockSpec(memory_space=pltpu.SMEM)] + [vmem_spec()] * 5,
        out_specs=vmem_spec(),
        compiler_params=params(),
        cost_estimate=pl.CostEstimate(
            flops=3 * rows * columns, bytes_accessed=8 * rows * columns, transcendentals=0
        ),
        name="to_slots",
    )(owners, own, *lower, *upper)


def update_kernel(rows_of, blocks, left_roots, right_roots, *outs):
    for slot in range(left_roots.shape[0]):
        block = blocks[rows_of[slot]]
        applied = jnp.dot(left_roots[slot], block, preferred_element_type=jnp.float32)
        product = jnp.dot(
            applied.astype(jnp.bfloat16), right_roots[slot], preferred_element_type=jnp.float32
        ).astype(jnp.bfloat16)
        product = product.reshape(outs[0].shape[1], -1, product.shape[1])
        start = 0
        for out in outs:
            out[rows_of[slot]] = product[:, start : start + out.shape[2]]
            start += out.shape[2]


def updates(rows_of, blocks, left_roots, right_roots, strips):
    capacity, block_size = left_roots.shape[0], left_roots.shape[1]
    return pl.pallas_call(
        update_kernel,
        out_shape=[
            jax.ShapeDtypeStruct((blocks.shape[0], strips, rows, block_size), jnp.bfloat16)
            for rows in BACKWARD
        ],
        in_specs=[pl.BlockSpec(memory_space=pltpu.SMEM)] + [vmem_spec()] * 3,
        out_specs=[vmem_spec()] * len(BACKWARD),
        compiler_params=params(),
        cost_estimate=pl.CostEstimate(
            flops=4 * capacity * block_size**3,
            bytes_accessed=8 * capacity * block_size**2,
            transcendentals=0,
        ),
        name="updates",
    )(rows_of, blocks, left_roots, right_roots)


def gram_kernel(rows_of, named, blocks, left, right, new_left, new_right):
    block = blocks[0]
    holds = named[pl.program_id(0)] > 0
    scale = 0.1 / block.shape[0]
    gram = lax.dot_general(block, block, (((1,), (1,)), ((), ())), preferred_element_type=jnp.float32)
    new_left[0] = 0.9 * left[0] + jnp.where(holds, scale * gram, 0.0)
    gram = lax.dot_general(block, block, (((0,), (0,)), ((), ())), preferred_element_type=jnp.float32)
    new_right[0] = 0.9 * right[0] + jnp.where(holds, scale * gram, 0.0)


def statistics(rows_of, named, blocks, factor_left, factor_right):
    capacity, block_size = factor_left.shape[0], factor_left.shape[1]
    at_row = lambda t, rows_of, named: (rows_of[t], 0, 0)
    square = pl.BlockSpec((1, block_size, block_size), lambda t, rows_of, named: (t, 0, 0))
    return pl.pallas_call(
        gram_kernel,
        grid_spec=pltpu.PrefetchScalarGridSpec(
            num_scalar_prefetch=2,
            grid=(capacity,),
            in_specs=[pl.BlockSpec((1, block_size, block_size), at_row), square, square],
            out_specs=[square, square],
        ),
        out_shape=[jax.ShapeDtypeStruct(factor_left.shape, jnp.float32)] * 2,
        compiler_params=params(),
        cost_estimate=pl.CostEstimate(
            flops=AHEAD,
            bytes_accessed=18 * capacity * block_size**2,
            transcendentals=0,
        ),
        name="statistics",
    )(
        rows_of,
        named,
        blocks,
        pltpu.with_memory_space_constraint(factor_left, pltpu.HBM),
        pltpu.with_memory_space_constraint(factor_right, pltpu.HBM),
    )


def pick_kernel(block_size, owners, slots, *refs):
    low, high = refs[-2:]
    count = low.shape[1] // block_size
    for at in range(2 * count):
        out, first = (low, at) if at < count else (high, at - count)
        out[:, first * block_size : (first + 1) * block_size] = slots[owners[at]]


def from_slots(owners, slots, after=(), flops=0):
    count = owners.shape[0] // 2
    _, rows, block_size = slots.shape
    return pl.pallas_call(
        functools.partial(pick_kernel, block_size),
        out_shape=[jax.ShapeDtypeStruct((rows, count * block_size), jnp.bfloat16)] * 2,
        in_specs=[pl.BlockSpec(memory_space=pltpu.SMEM), vmem_spec()]
        + [pl.BlockSpec(memory_space=pltpu.HBM)] * len(after),
        out_specs=[vmem_spec()] * 2,
        compiler_params=params(),
        cost_estimate=pl.CostEstimate(
            flops=flops, bytes_accessed=8 * rows * count * block_size, transcendentals=0
        ),
        name="from_slots",
    )(owners, slots, *(pltpu.with_memory_space_constraint(a, pltpu.HBM) for a in after))


def place_kernel(start, groups, *refs):
    pieces, out, sems = refs[: 2 * groups.shape[0]], refs[-2], refs[-1]
    rows, half = pieces[0].shape
    copies = []
    for at, piece in enumerate(pieces):
        first = pl.multiple_of(groups[at // 2] * (2 * half) + at % 2 * half, 128)
        where = out.at[pl.ds(start, rows), pl.ds(first, half)]
        copy = pltpu.make_async_copy(piece, where, sems.at[at])
        copy.start()
        copies.append(copy)
    for copy in copies:
        copy.wait()


def place(groups, pieces, start, shape, held):
    return pl.pallas_call(
        functools.partial(place_kernel, start),
        out_shape=jax.ShapeDtypeStruct(shape, jnp.bfloat16),
        in_specs=[pl.BlockSpec(memory_space=pltpu.SMEM)]
        + [vmem_spec()] * len(pieces)
        + [any_spec()] * len(held),
        out_specs=any_spec(),
        scratch_shapes=[pltpu.SemaphoreType.DMA((len(pieces),))],
        input_output_aliases={1 + len(pieces): 0} if held else {},
        compiler_params=params(),
        cost_estimate=pl.CostEstimate(
            flops=0,
            bytes_accessed=4 * len(pieces) * pieces[0].shape[0] * pieces[0].shape[1],
            transcendentals=0,
        ),
        name="place",
    )(groups, *pieces, *held)


def body(grads, owner_map, factor_left, factor_right, left_inverse_roots, right_inverse_roots):
    num_replicas = lax.axis_size("replica")
    num_shards = lax.axis_size("shard")
    replica_at = lax.axis_index("replica")
    shard_at = lax.axis_index("shard")
    strip_rows, columns = grads.shape[1], grads.shape[2]
    capacity, block_size = factor_left.shape[1], factor_left.shape[2]
    block_rows, block_cols = owner_map.shape
    per_group = block_cols // num_replicas
    width = per_group * block_size
    strips = block_size // strip_rows
    onward = [(at, (at + 1) % num_replicas) for at in range(num_replicas)]
    back = [(at, (at - 1) % num_replicas) for at in range(num_replicas)]
    to_right = lambda a: lax.ppermute(a, "replica", onward)
    to_left = lambda a: lax.ppermute(a, "replica", back)
    right_at = (replica_at + 1) % num_replicas
    left_at = (replica_at + num_replicas - 1) % num_replicas
    far_at = (replica_at + 2) % num_replicas

    group_entries = lax.dynamic_slice_in_dim(owner_map, replica_at * per_group, per_group, 1)
    row_entries = lax.dynamic_index_in_dim(group_entries, shard_at // strips, 0, keepdims=False)
    owners = row_entries // capacity
    targets = shard_at * capacity + jnp.arange(capacity, dtype=jnp.int32)
    match = jnp.any(group_entries[None] == targets[:, None, None], axis=2)
    named = jnp.any(match, axis=1)
    unused = jnp.logical_not(jnp.any(match, axis=0))
    rank_slot = jnp.cumsum(jnp.logical_not(named).astype(jnp.int32))
    rank_row = jnp.cumsum(unused.astype(jnp.int32))
    spare = jnp.logical_and(
        jnp.logical_and(jnp.logical_not(named)[:, None], unused[None]),
        rank_slot[:, None] == rank_row[None],
    )
    chosen = jnp.logical_or(match, spare)
    rows_of = jnp.sum(
        jnp.where(chosen, jnp.arange(block_rows, dtype=jnp.int32)[None], 0), axis=1
    ).astype(jnp.int32)
    named = named.astype(jnp.int32)

    groups = jnp.stack([replica_at, left_at, right_at, far_at]).astype(jnp.int32)
    half = strip_rows // 2
    far = cut(groups, grads, ((3, 0, half), (3, half, half)), width)
    passed_right, passed_left = to_right(far[0]), to_left(far[1])
    after, before = cut(groups, grads, ((2, half, half), (1, 0, half)), width, far)
    tile = 8
    view = grads[0].reshape(strip_rows // tile, tile, num_replicas, width).transpose(0, 2, 1, 3)

    def piece(group, start, rows):
        part = lax.dynamic_slice(
            view, (start // tile, group, 0, 0), (rows // tile, 1, tile, width)
        )
        return part.reshape(rows, width)

    ahead, behind = piece(right_at, 0, half), piece(left_at, half, half)
    own = piece(replica_at, 0, strip_rows)
    plain_right, plain_left = to_right(after), to_left(before)
    ahead, behind = relays(ahead, passed_right, behind, passed_left)
    added_right, added_left = to_right(ahead), to_left(behind)
    lower = (plain_left, added_right)
    upper = (added_left, plain_right)
    upper, rows_of, named, groups = lax.optimization_barrier((upper, rows_of, named, groups))
    slots = to_slots(owners, own, lower, upper, num_shards, block_size)
    came = lax.all_to_all(slots, "shard", split_axis=0, concat_axis=0, tiled=True)
    blocks = came.reshape(block_rows, block_size, block_size)
    outs = updates(rows_of, blocks, left_inverse_roots[0], right_inverse_roots[0], strips)
    new_left, new_right = statistics(rows_of, named, blocks, factor_left[0], factor_right[0])

    held, start, before = (), 0, None
    for out in outs:
        rows = out.shape[2]
        if before is not None:
            out, before = lax.optimization_barrier((out, before))
        returned = lax.all_to_all(
            out.reshape(num_shards, rows, block_size),
            "shard",
            split_axis=0,
            concat_axis=0,
            tiled=True,
        )
        low, high = from_slots(owners, returned, () if before is None else (new_left,))
        later, (low, high) = lax.optimization_barrier((owners, (low, high)))
        left_low, right_high = to_right(low), to_left(high)
        own_low, own_high = before = from_slots(later, returned)
        left_high, right_low = to_right(own_high), to_left(own_low)
        far_low, far_high = to_right(left_low), to_left(right_high)
        near = (own_low, own_high, left_low, left_high, right_low, right_high)
        held = (place(groups, near + (far_low, far_high), start, (strip_rows, columns), held),)
        start += rows
    (update,) = held
    return (new_left[None], new_right[None], update)


def solution(mesh):
    in_specs = (
        P("replica", "shard", None),
        P(),
        P(("replica", "shard"), None, None, None),
        P(("replica", "shard"), None, None, None),
        P(("replica", "shard"), None, None, None),
        P(("replica", "shard"), None, None, None),
    )
    out_specs = (
        P(("replica", "shard"), None, None, None),
        P(("replica", "shard"), None, None, None),
        P("shard", None),
    )
    return jax.shard_map(body, mesh=mesh, in_specs=in_specs, out_specs=out_specs, check_vma=False)
```

```python
import functools

import jax
import jax.numpy as jnp
from jax import lax
from jax.experimental import pallas as pl
from jax.experimental.pallas import tpu as pltpu
from jax.sharding import PartitionSpec as P

AHEAD = 30_000_000_000
BACKWARD = (48, 16)


def any_spec():
    return pl.BlockSpec(memory_space=pl.ANY)


def vmem_spec():
    return pl.BlockSpec(memory_space=pltpu.VMEM)


def params(mib=16):
    return pltpu.CompilerParams(vmem_limit_bytes=mib * 1024 * 1024)


def cut_kernel(cuts, groups, grads, *refs):
    outs, sems = refs[-1 - len(cuts) : -1], refs[-1]
    width = outs[0].shape[1]
    copies = []
    for at, (out, (group, start)) in enumerate(zip(outs, cuts, strict=True)):
        first = pl.multiple_of(groups[group] * width, 128)
        part = grads.at[0, pl.ds(start, out.shape[0]), pl.ds(first, width)]
        copy = pltpu.make_async_copy(part, out, sems.at[at])
        copy.start()
        copies.append(copy)
    for copy in copies:
        copy.wait()


def cut(groups, grads, cuts, width, after=()):
    total = sum(rows for _, _, rows in cuts) * width
    return pl.pallas_call(
        functools.partial(cut_kernel, [(group, start) for group, start, _ in cuts]),
        out_shape=[jax.ShapeDtypeStruct((rows, width), jnp.bfloat16) for _, _, rows in cuts],
        in_specs=[pl.BlockSpec(memory_space=pltpu.SMEM), pl.BlockSpec(memory_space=pltpu.HBM)]
        + [any_spec()] * len(after),
        out_specs=[vmem_spec()] * len(cuts),
        scratch_shapes=[pltpu.SemaphoreType.DMA((len(cuts),))],
        compiler_params=params(),
        cost_estimate=pl.CostEstimate(flops=0, bytes_accessed=4 * total, transcendentals=0),
        name="cut",
    )(groups, pltpu.with_memory_space_constraint(grads, pltpu.HBM), *after)


def relay_kernel(ahead, passed_right, behind, passed_left, out_right, out_left):
    for mine, passed, out in ((ahead, passed_right, out_right), (behind, passed_left, out_left)):
        out[...] = (mine[...].astype(jnp.float32) + passed[...].astype(jnp.float32)).astype(
            jnp.bfloat16
        )


def relays(ahead, passed_right, behind, passed_left):
    rows, columns = ahead.shape
    return pl.pallas_call(
        relay_kernel,
        out_shape=[jax.ShapeDtypeStruct((rows, columns), jnp.bfloat16)] * 2,
        in_specs=[vmem_spec()] * 4,
        out_specs=[vmem_spec()] * 2,
        compiler_params=params(),
        cost_estimate=pl.CostEstimate(
            flops=AHEAD, bytes_accessed=12 * rows * columns, transcendentals=0
        ),
        name="relays",
    )(ahead, passed_right, behind, passed_left)


def slot_kernel(block_size, owners, own, low_a, low_b, high_a, high_b, out):
    half = own.shape[0] // 2
    for at in range(own.shape[1] // block_size):
        columns = slice(at * block_size, (at + 1) * block_size)
        for first, one, other in ((0, low_a, low_b), (half, high_a, high_b)):
            total = (
                own[first : first + half, columns].astype(jnp.float32)
                + one[:, columns].astype(jnp.float32)
                + other[:, columns].astype(jnp.float32)
            )
            out[owners[at], first : first + half] = total.astype(jnp.bfloat16)


def to_slots(owners, own, lower, upper, num_shards, block_size):
    rows, columns = own.shape
    return pl.pallas_call(
        functools.partial(slot_kernel, block_size),
        out_shape=jax.ShapeDtypeStruct((num_shards, rows, block_size), jnp.bfloat16),
        in_specs=[pl.BlockSpec(memory_space=pltpu.SMEM)] + [vmem_spec()] * 5,
        out_specs=vmem_spec(),
        compiler_params=params(),
        cost_estimate=pl.CostEstimate(
            flops=3 * rows * columns, bytes_accessed=8 * rows * columns, transcendentals=0
        ),
        name="to_slots",
    )(owners, own, *lower, *upper)


def update_kernel(rows_of, blocks, left_roots, right_roots, *outs):
    for slot in range(left_roots.shape[0]):
        block = blocks[rows_of[slot]]
        applied = jnp.dot(left_roots[slot], block, preferred_element_type=jnp.float32)
        product = jnp.dot(
            applied.astype(jnp.bfloat16), right_roots[slot], preferred_element_type=jnp.float32
        ).astype(jnp.bfloat16)
        product = product.reshape(outs[0].shape[1], -1, product.shape[1])
        start = 0
        for out in outs:
            out[rows_of[slot]] = product[:, start : start + out.shape[2]]
            start += out.shape[2]


def updates(rows_of, blocks, left_roots, right_roots, strips):
    capacity, block_size = left_roots.shape[0], left_roots.shape[1]
    return pl.pallas_call(
        update_kernel,
        out_shape=[
            jax.ShapeDtypeStruct((blocks.shape[0], strips, rows, block_size), jnp.bfloat16)
            for rows in BACKWARD
        ],
        in_specs=[pl.BlockSpec(memory_space=pltpu.SMEM)] + [vmem_spec()] * 3,
        out_specs=[vmem_spec()] * len(BACKWARD),
        compiler_params=params(),
        cost_estimate=pl.CostEstimate(
            flops=4 * capacity * block_size**3,
            bytes_accessed=8 * capacity * block_size**2,
            transcendentals=0,
        ),
        name="updates",
    )(rows_of, blocks, left_roots, right_roots)


def gram_kernel(rows_of, named, blocks, left, right, new_left, new_right, held, sides, ins, outs):
    capacity, size = held.shape[:2]
    scale = 0.1 / size
    factors, news = (left, right), (new_left, new_right)
    arrivals, leaving = [], []
    for slot in range(capacity):
        copies = [pltpu.make_async_copy(blocks.at[rows_of[slot]], held.at[slot], ins.at[slot, 2])]
        for side, factor in enumerate(factors):
            copies.append(
                pltpu.make_async_copy(factor.at[slot], sides.at[side, slot], ins.at[slot, side])
            )
        for copy in copies:
            copy.start()
        arrivals.append(copies)
    for slot, copies in enumerate(arrivals):
        copies[0].wait()
        block = held[slot]
        holds = named[slot] > 0
        for side, new in enumerate(news):
            axis = 1 - side
            gram = lax.dot_general(
                block, block, (((axis,), (axis,)), ((), ())), preferred_element_type=jnp.float32
            )
            copies[1 + side].wait()
            sides[side, slot] = 0.9 * sides[side, slot] + jnp.where(holds, scale * gram, 0.0)
            copy = pltpu.make_async_copy(sides.at[side, slot], new.at[slot], outs.at[slot, side])
            copy.start()
            leaving.append(copy)
    for copy in leaving:
        copy.wait()


def statistics(rows_of, named, blocks, factor_left, factor_right):
    capacity, block_size = factor_left.shape[0], factor_left.shape[1]
    smem, hbm = pl.BlockSpec(memory_space=pltpu.SMEM), pl.BlockSpec(memory_space=pltpu.HBM)
    arrays = [
        pltpu.with_memory_space_constraint(array, pltpu.HBM)
        for array in (blocks, factor_left, factor_right)
    ]
    return pl.pallas_call(
        gram_kernel,
        out_shape=[jax.ShapeDtypeStruct(factor_left.shape, jnp.float32)] * 2,
        in_specs=[smem, smem, hbm, hbm, hbm],
        out_specs=[any_spec(), any_spec()],
        scratch_shapes=[
            pltpu.VMEM((capacity, block_size, block_size), jnp.bfloat16),
            pltpu.VMEM((2, capacity, block_size, block_size), jnp.float32),
            pltpu.SemaphoreType.DMA((capacity, 3)),
            pltpu.SemaphoreType.DMA((capacity, 2)),
        ],
        compiler_params=params(),
        cost_estimate=pl.CostEstimate(
            flops=AHEAD,
            bytes_accessed=18 * capacity * block_size**2,
            transcendentals=0,
        ),
        name="statistics",
    )(rows_of, named, *arrays)


def pick_kernel(block_size, owners, slots, *refs):
    low, high = refs[-2:]
    count = low.shape[1] // block_size
    for at in range(2 * count):
        out, first = (low, at) if at < count else (high, at - count)
        out[:, first * block_size : (first + 1) * block_size] = slots[owners[at]]


def from_slots(owners, slots, after=(), flops=0):
    count = owners.shape[0] // 2
    _, rows, block_size = slots.shape
    return pl.pallas_call(
        functools.partial(pick_kernel, block_size),
        out_shape=[jax.ShapeDtypeStruct((rows, count * block_size), jnp.bfloat16)] * 2,
        in_specs=[pl.BlockSpec(memory_space=pltpu.SMEM), vmem_spec()]
        + [pl.BlockSpec(memory_space=pltpu.HBM)] * len(after),
        out_specs=[vmem_spec()] * 2,
        compiler_params=params(),
        cost_estimate=pl.CostEstimate(
            flops=flops, bytes_accessed=8 * rows * count * block_size, transcendentals=0
        ),
        name="from_slots",
    )(owners, slots, *(pltpu.with_memory_space_constraint(a, pltpu.HBM) for a in after))


def again_kernel(*refs):
    count = len(refs) // 2
    for given, out in zip(refs[:count], refs[count:], strict=True):
        out[...] = given[...]


def again(*arrays):
    return pl.pallas_call(
        again_kernel,
        out_shape=[jax.ShapeDtypeStruct(array.shape, jnp.bfloat16) for array in arrays],
        in_specs=[vmem_spec()] * len(arrays),
        out_specs=[vmem_spec()] * len(arrays),
        compiler_params=params(),
        cost_estimate=pl.CostEstimate(
            flops=0, bytes_accessed=4 * sum(array.size for array in arrays), transcendentals=0
        ),
        name="again",
    )(*arrays)


def place_kernel(start, groups, *refs):
    pieces, out, sems = refs[: 2 * groups.shape[0]], refs[-2], refs[-1]
    rows, half = pieces[0].shape
    copies = []
    for at, piece in enumerate(pieces):
        first = pl.multiple_of(groups[at // 2] * (2 * half) + at % 2 * half, 128)
        where = out.at[pl.ds(start, rows), pl.ds(first, half)]
        copy = pltpu.make_async_copy(piece, where, sems.at[at])
        copy.start()
        copies.append(copy)
    for copy in copies:
        copy.wait()


def place(groups, pieces, start, shape, held):
    return pl.pallas_call(
        functools.partial(place_kernel, start),
        out_shape=jax.ShapeDtypeStruct(shape, jnp.bfloat16),
        in_specs=[pl.BlockSpec(memory_space=pltpu.SMEM)]
        + [vmem_spec()] * len(pieces)
        + [any_spec()] * len(held),
        out_specs=any_spec(),
        scratch_shapes=[pltpu.SemaphoreType.DMA((len(pieces),))],
        input_output_aliases={1 + len(pieces): 0} if held else {},
        compiler_params=params(),
        cost_estimate=pl.CostEstimate(
            flops=0,
            bytes_accessed=4 * len(pieces) * pieces[0].shape[0] * pieces[0].shape[1],
            transcendentals=0,
        ),
        name="place",
    )(groups, *pieces, *held)


def body(grads, owner_map, factor_left, factor_right, left_inverse_roots, right_inverse_roots):
    num_replicas = lax.axis_size("replica")
    num_shards = lax.axis_size("shard")
    replica_at = lax.axis_index("replica")
    shard_at = lax.axis_index("shard")
    strip_rows, columns = grads.shape[1], grads.shape[2]
    capacity, block_size = factor_left.shape[1], factor_left.shape[2]
    block_rows, block_cols = owner_map.shape
    per_group = block_cols // num_replicas
    width = per_group * block_size
    strips = block_size // strip_rows
    onward = [(at, (at + 1) % num_replicas) for at in range(num_replicas)]
    back = [(at, (at - 1) % num_replicas) for at in range(num_replicas)]
    to_right = lambda a: lax.ppermute(a, "replica", onward)
    to_left = lambda a: lax.ppermute(a, "replica", back)
    right_at = (replica_at + 1) % num_replicas
    left_at = (replica_at + num_replicas - 1) % num_replicas
    far_at = (replica_at + 2) % num_replicas

    group_entries = lax.dynamic_slice_in_dim(owner_map, replica_at * per_group, per_group, 1)
    row_entries = lax.dynamic_index_in_dim(group_entries, shard_at // strips, 0, keepdims=False)
    owners = row_entries // capacity
    targets = shard_at * capacity + jnp.arange(capacity, dtype=jnp.int32)
    match = jnp.any(group_entries[None] == targets[:, None, None], axis=2)
    named = jnp.any(match, axis=1)
    unused = jnp.logical_not(jnp.any(match, axis=0))
    rank_slot = jnp.cumsum(jnp.logical_not(named).astype(jnp.int32))
    rank_row = jnp.cumsum(unused.astype(jnp.int32))
    spare = jnp.logical_and(
        jnp.logical_and(jnp.logical_not(named)[:, None], unused[None]),
        rank_slot[:, None] == rank_row[None],
    )
    chosen = jnp.logical_or(match, spare)
    rows_of = jnp.sum(
        jnp.where(chosen, jnp.arange(block_rows, dtype=jnp.int32)[None], 0), axis=1
    ).astype(jnp.int32)
    named = named.astype(jnp.int32)

    groups = jnp.stack([replica_at, left_at, right_at, far_at]).astype(jnp.int32)
    half = strip_rows // 2
    far = cut(groups, grads, ((3, 0, half), (3, half, half)), width)
    passed_right, passed_left = to_right(far[0]), to_left(far[1])
    after, before = cut(groups, grads, ((2, half, half), (1, 0, half)), width, far)
    tile = 8
    view = grads[0].reshape(strip_rows // tile, tile, num_replicas, width).transpose(0, 2, 1, 3)

    def piece(group, start, rows):
        part = lax.dynamic_slice(
            view, (start // tile, group, 0, 0), (rows // tile, 1, tile, width)
        )
        return part.reshape(rows, width)

    ahead, behind = piece(right_at, 0, half), piece(left_at, half, half)
    own = piece(replica_at, 0, strip_rows)
    plain_right, plain_left = to_right(after), to_left(before)
    ahead, behind = relays(ahead, passed_right, behind, passed_left)
    added_right, added_left = to_right(ahead), to_left(behind)
    lower = (plain_left, added_right)
    upper = (added_left, plain_right)
    upper, rows_of, named, groups = lax.optimization_barrier((upper, rows_of, named, groups))
    slots = to_slots(owners, own, lower, upper, num_shards, block_size)
    came = lax.all_to_all(slots, "shard", split_axis=0, concat_axis=0, tiled=True)
    blocks = came.reshape(block_rows, block_size, block_size)
    outs = updates(rows_of, blocks, left_inverse_roots[0], right_inverse_roots[0], strips)
    new_left, new_right = statistics(rows_of, named, blocks, factor_left[0], factor_right[0])

    held, start, before = (), 0, None
    for out in outs:
        rows = out.shape[2]
        if before is not None:
            out, before = lax.optimization_barrier((out, before))
            (out,) = again(out)
        returned = lax.all_to_all(
            out.reshape(num_shards, rows, block_size),
            "shard",
            split_axis=0,
            concat_axis=0,
            tiled=True,
        )
        low, high = from_slots(owners, returned, () if before is None else (new_left,))
        left_low, right_high = to_right(low), to_left(high)
        own_low, own_high = before = again(low, high)
        left_high, right_low = to_right(own_high), to_left(own_low)
        far_low, far_high = to_right(left_low), to_left(right_high)
        near = (own_low, own_high, left_low, left_high, right_low, right_high)
        held = (place(groups, near + (far_low, far_high), start, (strip_rows, columns), held),)
        start += rows
    (update,) = held
    return (new_left[None], new_right[None], update)


def solution(mesh):
    in_specs = (
        P("replica", "shard", None),
        P(),
        P(("replica", "shard"), None, None, None),
        P(("replica", "shard"), None, None, None),
        P(("replica", "shard"), None, None, None),
        P(("replica", "shard"), None, None, None),
    )
    out_specs = (
        P(("replica", "shard"), None, None, None),
        P(("replica", "shard"), None, None, None),
        P("shard", None),
    )
    return jax.shard_map(body, mesh=mesh, in_specs=in_specs, out_specs=out_specs, check_vma=False)
```
